128 devices in a mesh: layer: 4 (over z_lo, core), lat: 32 (over z_hi, y, x).
Axes of the slice: x: 4, y: 4, z: 4 (z_hi: 2, z_lo: 2; z = z_hi * 2 + z_lo), core: 2. Of those that a mesh axis runs over, the one named last changes fastest.
Arguments:
- resid: bfloat16 [4, 256, 4608], P('layer', None, 'lat'), may hold values from -6 to 6
- target: bfloat16 [4, 256, 4608], P('layer', None, 'lat'), may hold values from -6 to 6
- enc_weight: bfloat16 [4, 4608, 8192], P('layer', None, 'lat'), may hold values from -0.09375 to 0.09375
- enc_bias: float32 [4, 8192], P('layer', 'lat'), may hold values from -3 to 3
- dec_weight: bfloat16 [4, 4, 8192, 4608], P('layer', None, 'lat'), may hold values from -0.125 to 0.125
- dec_bias: float32 [4, 4608], P('layer', 'lat'), may hold values from -3 to 3
Outputs:
- grad_enc: bfloat16 [4, 4608, 8192], P('layer', None, 'lat')
- grad_enc_bias: float32 [4, 8192], P('layer', 'lat')
- grad_dec: bfloat16 [4, 4, 8192, 4608], P('layer', None, 'lat')
- grad_dec_bias: float32 [4, 4608], P('layer', 'lat')
The draws below stay inside these ranges and needn't reach their ends.
All inputs are finite; a program needn't handle non-finite values.
Results may differ from the reference program's by a relative error of at most 0.0085.
Values may be sent and summed in bfloat16 or wider, within the bound.
No kernel may reach another device: no remote copies, remote signals or barrier semaphores. Data moves between devices by JAX's collectives and lax.ppermute only.
A program may use at most 128 MiB of HBM per device.

```python
import jax
import jax.numpy as jnp
from jax import lax

D = 4608
F = 8192
TOK = 256
LAYERS = 4


def spiked(result, stream_key, source, target, shards_of, factor):
    owner, partner = [(jnp.arange(result.shape[position]) // (result.shape[position] // shards_of)).reshape([-1 if axis == position else 1 for axis in range(result.ndim)]) for position in (source, target)]
    chosen = jax.random.permutation(stream_key, shards_of)[partner]
    strong = (owner == chosen) | (owner == (partner + shards_of // 2) % shards_of)
    return jnp.where(strong, factor * result, result)


def steps_of(own_key, dims, split, smallest, top_value):
    factor_of, own = 1.0, jax.random.fold_in(own_key, 6)
    for axis_at, parts in split:
        heights = jnp.exp(jax.random.uniform(jax.random.fold_in(own, axis_at), (parts,), jnp.float32, smallest / len(split), top_value / len(split)))
        factor_of = factor_of * jnp.repeat(heights, dims[axis_at] // parts).reshape([-1 if axis == axis_at else 1 for axis in range(len(dims))])
    return factor_of


def gaussian(stream_key, extent, spread, most, split=(), kind=jnp.bfloat16):
    drawn = jax.random.normal(stream_key, extent, jnp.float32) * spread
    if len(split) > 0:
        drawn = steps_of(stream_key, extent, split, -0.22, 0.18) * drawn
    return jnp.clip(drawn, min=-most, max=most).astype(kind)


def noise_with(rng, shape, deviation, limit, cuts, heavy, held_as=jnp.bfloat16):
    result = deviation * jax.random.normal(rng, shape, jnp.float32)
    if cuts:
        result = result * steps_of(rng, shape, cuts, -0.22, 0.18)
    return jnp.clip(spiked(result, jax.random.fold_in(rng, 3), *heavy), -limit, limit).astype(held_as)


def setup_inputs(seed: int = 0) -> dict:
    seeds = jax.random.split(jax.random.key(seed), 7)
    resid = gaussian(seeds[0], (LAYERS, TOK, D), 1.0, 6.0, ((0, 4), (2, 32)))
    target = gaussian(seeds[1], (LAYERS, TOK, D), 1.0, 6.0, ((0, 4), (2, 32)))
    enc_weight = gaussian(seeds[2], (LAYERS, D, F), D ** -0.5, 0.09375, ((0, 4), (2, 32)))
    enc_bias = gaussian(seeds[3], (LAYERS, F), 0.5, 3.0, ((0, 4), (1, 32)), jnp.float32)
    dec_weight = noise_with(seeds[4], (LAYERS, LAYERS, F, D), F ** -0.5, 0.125, ((0, 4), (2, 32)), (2, 3, 32, 2.75))
    dec_bias = gaussian(seeds[5], (LAYERS, D), 0.5, 3.0, ((0, 4), (1, 32)), jnp.float32)
    return {"resid": resid, "target": target, "enc_weight": enc_weight, "enc_bias": enc_bias, "dec_weight": dec_weight, "dec_bias": dec_bias}


def gelu_tanh(values):
    return jax.nn.gelu(values, approximate=True)

def reference(resid, target, enc_weight, enc_bias, dec_weight, dec_bias):
    factor = 2.0 / TOK
    preacts = []
    latents = []
    for source in range(LAYERS):
        preact = jnp.dot(resid[source], enc_weight[source], preferred_element_type=jnp.float32) + enc_bias[source]
        preacts.append(preact)
        latents.append(gelu_tanh(preact).astype(jnp.bfloat16))
    out_grads = []
    bias_grads = []
    for target_idx in range(LAYERS):
        recon = jnp.zeros((TOK, D), jnp.float32)
        for source in range(target_idx + 1):
            recon = recon + jnp.dot(latents[source], dec_weight[source, target_idx], preferred_element_type=jnp.float32)
        error = recon + dec_bias[target_idx] - target[target_idx].astype(jnp.float32)
        bias_grads.append(factor * lax.optimization_barrier(jnp.sum(error, axis=0)))
        out_grads.append((factor * error).astype(jnp.bfloat16))
    enc_grads = []
    enc_bias_grads = []
    dec_grads = []
    for source in range(LAYERS):
        latent_grad = jnp.zeros((TOK, F), jnp.float32)
        row_grads = []
        for target_idx in range(LAYERS):
            if target_idx >= source:
                latent_grad = latent_grad + jnp.dot(out_grads[target_idx], dec_weight[source, target_idx].T, preferred_element_type=jnp.float32)
                row_grads.append(jnp.dot(latents[source].T, out_grads[target_idx], preferred_element_type=jnp.float32).astype(jnp.bfloat16))
            else:
                row_grads.append(jnp.zeros((F, D), jnp.bfloat16))
        dec_grads.append(jnp.stack(row_grads))
        _, backward = jax.vjp(gelu_tanh, preacts[source])
        pre_grad = backward(latent_grad)[0]
        enc_bias_grads.append(lax.optimization_barrier(jnp.sum(pre_grad, axis=0)))
        enc_grads.append(jnp.dot(resid[source].T, pre_grad.astype(jnp.bfloat16), preferred_element_type=jnp.float32).astype(jnp.bfloat16))
    return (jnp.stack(enc_grads), jnp.stack(enc_bias_grads), jnp.stack(dec_grads), jnp.stack(bias_grads))
```

```python
import jax
import jax.numpy as jnp
from jax import lax
from jax.sharding import Mesh, PartitionSpec as P

LAYER = ("zlo", "core")
LAT = ("zhi", "y", "x")
SAME_CORE = ("zlo", "zhi", "y", "x")


def gelu_tanh(values):
    return jax.nn.gelu(values, approximate=True)


def dot(a, b, ca, cb):
    return lax.dot_general(a, b, (((ca,), (cb,)), ((), ())), preferred_element_type=jnp.float32)


def gather_rows(block, axes, count):
    copies = jnp.broadcast_to(block[None], (count,) + block.shape)
    return lax.all_to_all(copies, axes, 0, 0, tiled=True)


def body(resid, target, enc_weight, enc_bias, dec_weight, dec_bias):
    zlo, core = lax.axis_index("zlo"), lax.axis_index("core")
    tokens = resid.shape[1]
    own_rows = resid.shape[2]
    lats = lax.axis_size("zhi") * lax.axis_size("y") * lax.axis_size("x")
    width = own_rows * lats
    factor = 2.0 / tokens
    dec = dec_weight[0]

    resid_t = gather_rows(resid[0].T, LAT, lats).reshape(width, tokens)
    preact = dot(enc_weight[0], resid_t, 0, 0) + enc_bias[0][:, None]
    latent = gelu_tanh(preact).astype(jnp.bfloat16)

    def partial(t):
        return dot(lax.dynamic_index_in_dim(dec, t, 0, keepdims=False), latent, 0, 0)

    give_late = partial(3 - core).astype(jnp.bfloat16)
    got_late = lax.ppermute(give_late, LAYER, [(0, 1), (1, 0), (2, 3)])
    give_early = partial(1 - core).astype(jnp.bfloat16)
    got_early = lax.ppermute(give_early, LAYER, [(0, 1)])
    early = partial(core) + got_early.astype(jnp.float32)
    early = jnp.where(zlo == 0, early, 0.0).astype(jnp.bfloat16)
    late = (partial(2 + core) + got_late.astype(jnp.float32)).astype(jnp.bfloat16)
    sums = jnp.stack([early, late]).reshape(2 * lats, own_rows, tokens)
    parts = lax.all_to_all(sums, SAME_CORE, 0, 0, tiled=True)
    recon = jnp.sum(parts.astype(jnp.float32), axis=0)

    error = recon + dec_bias[0][:, None] - target[0].T.astype(jnp.float32)
    grad_dec_bias = (factor * jnp.sum(error, axis=1))[None]
    out_grad = (factor * error).astype(jnp.bfloat16)

    grads = gather_rows(out_grad, SAME_CORE, 2 * lats).reshape(2, width, tokens)
    got_late_grad = lax.ppermute(grads[1], LAYER, [(0, 1), (1, 0), (3, 2)])
    got_early_grad = lax.ppermute(grads[0], LAYER, [(1, 0)])
    layer = 2 * zlo + core
    first, second = jnp.where(core == 0, grads[0], got_early_grad), jnp.where(core == 0, got_early_grad, grads[0])
    third, fourth = jnp.where(core == 0, grads[1], got_late_grad), jnp.where(core == 0, got_late_grad, grads[1])
    latent_grad = 0.0
    grad_dec = []
    for t, grad in enumerate((first, second, third, fourth)):
        grad = jnp.where(t >= layer, grad, jnp.zeros_like(grad))
        latent_grad = latent_grad + dot(dec[t], grad, 1, 0)
        grad_dec.append(dot(latent, grad, 1, 1).astype(jnp.bfloat16))
    grad_dec = jnp.stack(grad_dec)[None]

    _, backward = jax.vjp(gelu_tanh, preact)
    pre_grad = backward(latent_grad)[0]
    grad_enc_bias = jnp.sum(pre_grad, axis=1)[None]
    grad_enc = dot(resid_t, pre_grad.astype(jnp.bfloat16), 1, 1).astype(jnp.bfloat16)[None]
    return (grad_enc, grad_enc_bias, grad_dec, grad_dec_bias)


def solution(mesh):
    fine = Mesh(mesh.devices.reshape(2, 2, 2, 4, 4), LAYER + LAT)
    in_specs = (
        P(LAYER, None, LAT),
        P(LAYER, None, LAT),
        P(LAYER, None, LAT),
        P(LAYER, LAT),
        P(LAYER, None, LAT, None),
        P(LAYER, LAT),
    )
    out_specs = (
        P(LAYER, None, LAT),
        P(LAYER, LAT),
        P(LAYER, None, LAT, None),
        P(LAYER, LAT),
    )
    return jax.shard_map(body, mesh=fine, in_specs=in_specs, out_specs=out_specs, check_vma=False)
```

```python
import math

import jax
import jax.numpy as jnp
from jax import lax
from jax.experimental import pallas as pl
from jax.experimental.pallas import tpu as pltpu
from jax.sharding import Mesh, PartitionSpec as P

LAYER = ("zlo", "core")
LAT = ("zhi", "y", "x")
SAME_CORE = ("zlo", "zhi", "y", "x")


def gelu_tanh(values):
    return jax.nn.gelu(values, approximate=True)


def dot(a, b, ca, cb):
    return lax.dot_general(a, b, (((ca,), (cb,)), ((), ())), preferred_element_type=jnp.float32)


def gather_rows(block, axes, count):
    copies = jnp.broadcast_to(block[None], (count,) + block.shape)
    return lax.all_to_all(copies, axes, 0, 0, tiled=True)


def gelu_slope(x):
    scale, cubic = math.sqrt(2.0 / math.pi), 0.044715
    bent = jnp.tanh(scale * (x + cubic * x * x * x))
    return 0.5 * (1.0 + bent) + 0.5 * x * (1.0 - bent * bent) * scale * (1.0 + 3.0 * cubic * x * x)


def slot_step(plan, dec_ref, early_ref, late_ref, latent_ref, grad_dec_ref, total_ref):
    slot = pl.program_id(0)
    live = plan[2 * slot + 1] == 1

    def work(grad_ref):
        grad = grad_ref[...]
        total_ref[...] += dot(dec_ref[0], grad, 1, 0)
        grad_dec_ref[0] = dot(latent_ref[...], grad, 1, 1).astype(jnp.bfloat16)

    pl.when(live & (slot == 0))(lambda: work(early_ref))
    pl.when(live & (slot == 1))(lambda: work(late_ref))

    @pl.when(jnp.logical_not(live))
    def _():
        grad_dec_ref[...] = jnp.zeros_like(grad_dec_ref)


def own_kernel(plan, dec_ref, early_ref, late_ref, latent_ref, grad_dec_ref, total_ref):
    @pl.when((pl.program_id(0) == 0) & (pl.program_id(1) == 0))
    def _():
        total_ref[...] = jnp.zeros_like(total_ref)

    slot_step(plan, dec_ref, early_ref, late_ref, latent_ref, grad_dec_ref, total_ref)


def other_kernel(plan, dec_ref, early_ref, late_ref, latent_ref, start_ref, preact_ref, _, grad_dec_ref, pre_ref,
                 bias_ref, total_ref):
    slot, tile = pl.program_id(0), pl.program_id(1)

    @pl.when((slot == 0) & (tile == 0))
    def _():
        total_ref[...] = start_ref[...]

    slot_step(plan, dec_ref, early_ref, late_ref, latent_ref, grad_dec_ref, total_ref)

    @pl.when((slot == 1) & (tile == pl.num_programs(1) - 1))
    def _():
        pre_grad = total_ref[...] * gelu_slope(preact_ref[...])
        bias_ref[...] = jnp.sum(pre_grad, axis=1, keepdims=True)
        pre_ref[...] = pre_grad.astype(jnp.bfloat16)


TILE = 1152
PARAMS = dict(dimension_semantics=("arbitrary", "arbitrary"), vmem_limit_bytes=32 * 1024 * 1024)


def slot_specs(rows, tokens, width):
    tiles = width // TILE

    def dec_map(slot, tile, plan):
        return plan[2 * slot], 0, tile * plan[2 * slot + 1]

    dec_spec = pl.BlockSpec((1, rows, TILE), dec_map)
    early_spec = pl.BlockSpec(
        (TILE, tokens), lambda slot, tile, plan: (jnp.where(slot == 0, tile, tiles - 1) * plan[1], 0))
    late_spec = pl.BlockSpec((TILE, tokens), lambda slot, tile, plan: (jnp.where(slot == 0, 0, tile) * plan[3], 0))
    out_spec = pl.BlockSpec((1, rows, TILE), lambda slot, tile, plan: (plan[2 * slot], 0, tile))
    return tiles, dec_spec, early_spec, late_spec, out_spec


def whole(*shape):
    return pl.BlockSpec(shape, lambda slot, tile, plan: (0,) * len(shape))


def cost(dec):
    _, rows, width = dec.shape
    return pl.CostEstimate(flops=8 * rows * width * 256, bytes_accessed=6 * rows * width * 2, transcendentals=0)


def backward_own(plan, dec, early, late, latent):
    _, rows, width = dec.shape
    tokens = latent.shape[1]
    tiles, dec_spec, early_spec, late_spec, out_spec = slot_specs(rows, tokens, width)
    return pl.pallas_call(
        own_kernel,
        grid_spec=pltpu.PrefetchScalarGridSpec(
            num_scalar_prefetch=1,
            grid=(2, tiles),
            in_specs=[dec_spec, early_spec, late_spec, whole(rows, tokens)],
            out_specs=[out_spec, whole(rows, tokens)],
        ),
        out_shape=[jax.ShapeDtypeStruct(dec.shape, jnp.bfloat16), jax.ShapeDtypeStruct((rows, tokens), jnp.float32)],
        compiler_params=pltpu.CompilerParams(**PARAMS),
        cost_estimate=cost(dec),
        name="backward_own",
    )(plan, dec, early, late, latent)


def backward_other(plan, dec, early, late, latent, start, preact, grad_dec):
    _, rows, width = dec.shape
    tokens = latent.shape[1]
    tiles, dec_spec, early_spec, late_spec, out_spec = slot_specs(rows, tokens, width)
    return pl.pallas_call(
        other_kernel,
        grid_spec=pltpu.PrefetchScalarGridSpec(
            num_scalar_prefetch=1,
            grid=(2, tiles),
            in_specs=[dec_spec, early_spec, late_spec, whole(rows, tokens), whole(rows, tokens), whole(rows, tokens),
                      pl.BlockSpec(memory_space=pl.ANY)],
            out_specs=[out_spec, whole(rows, tokens), whole(rows, 1)],
            scratch_shapes=[pltpu.VMEM((rows, tokens), jnp.float32)],
        ),
        out_shape=[
            jax.ShapeDtypeStruct(dec.shape, jnp.bfloat16),
            jax.ShapeDtypeStruct((rows, tokens), jnp.bfloat16),
            jax.ShapeDtypeStruct((rows, 1), jnp.float32),
        ],
        input_output_aliases={7: 0},
        compiler_params=pltpu.CompilerParams(**PARAMS),
        cost_estimate=cost(dec),
        name="backward_other",
    )(plan, dec, early, late, latent, start, preact, grad_dec)


def body(resid, target, enc_weight, enc_bias, dec_weight, dec_bias):
    zlo, core = lax.axis_index("zlo"), lax.axis_index("core")
    tokens = resid.shape[1]
    own_rows = resid.shape[2]
    lats = lax.axis_size("zhi") * lax.axis_size("y") * lax.axis_size("x")
    width = own_rows * lats
    factor = 2.0 / tokens
    dec = dec_weight[0]

    resid_t = gather_rows(resid[0].T, LAT, lats).reshape(width, tokens)
    preact = dot(enc_weight[0], resid_t, 0, 0) + enc_bias[0][:, None]
    latent = gelu_tanh(preact).astype(jnp.bfloat16)

    def partial(t):
        return dot(lax.dynamic_index_in_dim(dec, t, 0, keepdims=False), latent, 0, 0)

    give_late = partial(3 - core).astype(jnp.bfloat16)
    got_late = lax.ppermute(give_late, LAYER, [(0, 1), (1, 0), (2, 3)])
    give_early = partial(1 - core).astype(jnp.bfloat16)
    got_early = lax.ppermute(give_early, LAYER, [(0, 1)])
    early = partial(core) + got_early.astype(jnp.float32)
    early = jnp.where(zlo == 0, early, 0.0).astype(jnp.bfloat16)
    late = (partial(2 + core) + got_late.astype(jnp.float32)).astype(jnp.bfloat16)
    sums = jnp.stack([early, late]).reshape(2 * lats, own_rows, tokens)
    parts = lax.all_to_all(sums, SAME_CORE, 0, 0, tiled=True)
    recon = jnp.sum(parts.astype(jnp.float32), axis=0)

    error = recon + dec_bias[0][:, None] - target[0].T.astype(jnp.float32)
    grad_dec_bias = (factor * jnp.sum(error, axis=1))[None]
    out_grad = (factor * error).astype(jnp.bfloat16)

    grads = gather_rows(out_grad, SAME_CORE, 2 * lats).reshape(2, width, tokens)
    got_late_grad = lax.ppermute(grads[1], LAYER, [(0, 1), (1, 0), (3, 2)])
    got_early_grad = lax.ppermute(grads[0], LAYER, [(1, 0)])

    on = jnp.int32(1)
    own_plan = jnp.stack([core, (zlo == 0).astype(jnp.int32), 2 + core, on])
    other_plan = jnp.stack([1 - core, ((zlo == 0) & (core == 0)).astype(jnp.int32),
                            3 - core, ((zlo == 0) | (core == 0)).astype(jnp.int32)])
    grad_dec, latent_grad = backward_own(own_plan, dec, grads[0], grads[1], latent)
    grad_dec, pre_grad, bias_grad = backward_other(
        other_plan, dec, got_early_grad, got_late_grad, latent, latent_grad, preact, grad_dec)
    grad_enc = dot(resid_t, pre_grad, 1, 1).astype(jnp.bfloat16)[None]
    return (grad_enc, bias_grad.reshape(1, -1), grad_dec[None], grad_dec_bias)


def solution(mesh):
    fine = Mesh(mesh.devices.reshape(2, 2, 2, 4, 4), LAYER + LAT)
    in_specs = (
        P(LAYER, None, LAT),
        P(LAYER, None, LAT),
        P(LAYER, None, LAT),
        P(LAYER, LAT),
        P(LAYER, None, LAT, None),
        P(LAYER, LAT),
    )
    out_specs = (
        P(LAYER, None, LAT),
        P(LAYER, LAT),
        P(LAYER, None, LAT, None),
        P(LAYER, LAT),
    )
    return jax.shard_map(body, mesh=fine, in_specs=in_specs, out_specs=out_specs, check_vma=False)
```

```python
import math

import jax
import jax.numpy as jnp
from jax import lax
from jax.experimental import pallas as pl
from jax.experimental.pallas import tpu as pltpu
from jax.sharding import Mesh, PartitionSpec as P

LAYER = ("zlo", "core")
LAT = ("zhi", "y", "x")
SAME_CORE = ("zlo", "zhi", "y", "x")
TILE = 1152
AHEAD = 3
ANYWHERE = pl.BlockSpec(memory_space=pl.ANY)
LOCAL = pl.BlockSpec(memory_space=pltpu.VMEM)
PARAMS = pltpu.CompilerParams(vmem_limit_bytes=60 * 1024 * 1024)


def gelu_tanh(values):
    return jax.nn.gelu(values, approximate=True)


def gelu_slope(x):
    scale, cubic = math.sqrt(2.0 / math.pi), 0.044715
    bent = jnp.tanh(scale * (x + cubic * x * x * x))
    return 0.5 * (1.0 + bent) + 0.5 * x * (1.0 - bent * bent) * scale * (1.0 + 3.0 * cubic * x * x)


def dot(a, b, ca, cb):
    return lax.dot_general(a, b, (((ca,), (cb,)), ((), ())), preferred_element_type=jnp.float32)


def gather_rows(block, axes, count):
    copies = jnp.broadcast_to(block[None], (count,) + block.shape)
    return lax.all_to_all(copies, axes, 0, 0, tiled=True)


def buffers(count, *shape):
    return [pltpu.VMEM((count,) + shape, jnp.bfloat16), pltpu.SemaphoreType.DMA((count,))]


def place():
    return lax.axis_index("zlo"), lax.axis_index("core")


def decode(dec, lent, latent, lent_latent):
    _, rows, width = dec.shape
    tokens = latent.shape[1]
    tiles = width // TILE
    steps = 2 * tiles

    def kernel(dec_ref, lent_ref, latent_ref, lent_latent_ref, sums_ref,
               own_buf, own_sem, lent_buf, lent_sem, out_buf, out_sem):
        zlo, core = place()

        def live(step):
            return (zlo == 0) | (step >= tiles)

        def lent_live(step):
            return (core == 1) | (zlo == 0) if step >= tiles else (core == 1) & (zlo == 0)

        def source(ref, step):
            return ref.at[core + 2 * (step // tiles), :, pl.ds(step % tiles * TILE, TILE)]

        def own_copy(step):
            return pltpu.make_async_copy(source(dec_ref, step), own_buf.at[step], own_sem.at[step])

        def lent_copy(step):
            return pltpu.make_async_copy(source(lent_ref, step), lent_buf.at[step], lent_sem.at[step])

        def out_copy(step):
            block = sums_ref.at[step // tiles, pl.ds(step % tiles * TILE, TILE)]
            return pltpu.make_async_copy(out_buf.at[step], block, out_sem.at[step])

        def begin(step):
            @pl.when(live(step))
            def _():
                own_copy(step).start()

            @pl.when(lent_live(step))
            def _():
                lent_copy(step).start()

        for step in range(AHEAD):
            begin(step)
        for step in range(steps):
            if step + AHEAD < steps:
                begin(step + AHEAD)

            @pl.when(live(step))
            def _(step=step):
                own_copy(step).wait()
                own = dot(own_buf[step], latent_ref[...], 0, 0)

                @pl.when(lent_live(step))
                def _():
                    lent_copy(step).wait()
                    both = own + dot(lent_buf[step], lent_latent_ref[...], 0, 0)
                    out_buf[step] = both.astype(jnp.bfloat16)

                @pl.when(jnp.logical_not(lent_live(step)))
                def _():
                    out_buf[step] = own.astype(jnp.bfloat16)

            @pl.when(jnp.logical_not(live(step)))
            def _(step=step):
                out_buf[step] = jnp.zeros((TILE, tokens), jnp.bfloat16)

            out_copy(step).start()
        for step in range(steps):
            out_copy(step).wait()

    return pl.pallas_call(
        kernel,
        in_specs=[ANYWHERE, ANYWHERE, LOCAL, LOCAL],
        out_specs=ANYWHERE,
        scratch_shapes=buffers(steps, rows, TILE) * 2 + buffers(steps, TILE, tokens),
        out_shape=jax.ShapeDtypeStruct((2, width, tokens), jnp.bfloat16),
        compiler_params=PARAMS,
        cost_estimate=pl.CostEstimate(
            flops=8 * rows * width * tokens, bytes_accessed=12 * rows * width, transcendentals=0),
        name="decode",
    )(dec, lent, latent, lent_latent)


def backward(dec, latent, grads, given=None, finish=None):
    _, rows, width = dec.shape
    tokens = latent.shape[1]
    tiles = width // TILE
    steps = 2 * tiles
    given = given or []
    n_given = len(given)

    def kernel(dec_ref, latent_ref, grads_ref, *refs):
        zlo, core = place()
        first_target = 1 - core if given else core
        given_refs, refs = refs[:n_given], refs[n_given:]
        if finish:
            preact_ref, resid_ref, grad_dec_ref, grad_enc_ref, bias_ref, *refs = refs
            total_ref, resid_buf, resid_sem, enc_buf, enc_sem, *refs = refs
        else:
            grad_dec_ref, total_ref, *refs = refs
        dec_buf, dec_sem, grad_buf, grad_sem, out_buf, out_sem = refs

        def target(step):
            return first_target + 2 * (step // tiles)

        def live(step):
            return target(step) >= 2 * zlo + core

        def columns(step):
            return pl.ds(step % tiles * TILE, TILE)

        def dec_copy(step):
            source = dec_ref.at[target(step), :, columns(step)]
            return pltpu.make_async_copy(source, dec_buf.at[step], dec_sem.at[step])

        def grad_copy(step):
            source = grads_ref.at[step // tiles, columns(step)]
            return pltpu.make_async_copy(source, grad_buf.at[step], grad_sem.at[step])

        def out_copy(step):
            block = grad_dec_ref.at[target(step), :, columns(step)]
            return pltpu.make_async_copy(out_buf.at[step], block, out_sem.at[step])

        def resid_copy(part):
            return pltpu.make_async_copy(resid_ref.at[columns(part)], resid_buf.at[part], resid_sem.at[part])

        def enc_copy(part):
            return pltpu.make_async_copy(enc_buf.at[part], grad_enc_ref.at[columns(part)], enc_sem.at[part])

        def begin(step):
            @pl.when(live(step))
            def _():
                grad_copy(step).start()
                dec_copy(step).start()

        for step in range(AHEAD):
            begin(step)
        total_ref[...] = given_refs[0][...] if given else jnp.zeros_like(total_ref)
        for step in range(steps):
            if step + AHEAD < steps:
                begin(step + AHEAD)
            elif finish and step + AHEAD < steps + tiles:
                resid_copy(step + AHEAD - steps).start()

            @pl.when(live(step))
            def _(step=step):
                grad_copy(step).wait()
                dec_copy(step).wait()
                grad = grad_buf[step]
                total_ref[...] += dot(dec_buf[step], grad, 1, 0)
                out_buf[step] = dot(latent_ref[...], grad, 1, 1).astype(jnp.bfloat16)

            @pl.when(jnp.logical_not(live(step)))
            def _(step=step):
                out_buf[step] = jnp.zeros((rows, TILE), jnp.bfloat16)

            out_copy(step).start()
        if finish:
            for part in range(AHEAD, tiles):
                resid_copy(part).start()
            pre_grad = total_ref[...] * gelu_slope(preact_ref[...])
            bias_ref[...] = jnp.sum(pre_grad.T, axis=0, keepdims=True)
            pre_grad = pre_grad.astype(jnp.bfloat16)
            for part in range(tiles):
                resid_copy(part).wait()
                enc_buf[part] = dot(resid_buf[part], pre_grad, 1, 1).astype(jnp.bfloat16)
                enc_copy(part).start()
        for step in range(steps):
            out_copy(step).wait()
        if finish:
            for part in range(tiles):
                enc_copy(part).wait()

    operands = [dec, latent, grads, *given]
    in_specs = [ANYWHERE, LOCAL, ANYWHERE] + [LOCAL, ANYWHERE][:n_given]
    out_shape = [jax.ShapeDtypeStruct(dec.shape, jnp.bfloat16)]
    out_specs = [ANYWHERE]
    scratch = []
    if finish:
        operands += finish
        in_specs += [LOCAL, ANYWHERE]
        out_shape += [jax.ShapeDtypeStruct((width, rows), jnp.bfloat16), jax.ShapeDtypeStruct((1, rows), jnp.float32)]
        out_specs += [ANYWHERE, LOCAL]
        scratch = [pltpu.VMEM((rows, tokens), jnp.float32)] + buffers(tiles, TILE, tokens) + buffers(tiles, TILE, rows)
    else:
        out_shape += [jax.ShapeDtypeStruct((rows, tokens), jnp.float32)]
        out_specs += [LOCAL]
    scratch += buffers(steps, rows, TILE) + buffers(steps, TILE, tokens) + buffers(steps, rows, TILE)
    return pl.pallas_call(
        kernel,
        in_specs=in_specs,
        out_specs=out_specs,
        scratch_shapes=scratch,
        out_shape=out_shape,
        input_output_aliases={4: 0} if given else {},
        compiler_params=PARAMS,
        cost_estimate=pl.CostEstimate(
            flops=8 * rows * width * tokens, bytes_accessed=12 * rows * width, transcendentals=0),
        name="other_targets" if given else "own_targets",
    )(*operands)


def body(resid, target, enc_weight, enc_bias, dec_weight, dec_bias):
    tokens = resid.shape[1]
    own_rows = resid.shape[2]
    lats = lax.axis_size("zhi") * lax.axis_size("y") * lax.axis_size("x")
    width = own_rows * lats
    factor = 2.0 / tokens
    dec = dec_weight[0]

    lent = lax.ppermute(dec, LAYER, [(0, 1), (1, 0), (2, 3)])

    resid_t = gather_rows(resid[0].T, LAT, lats).reshape(width, tokens)
    resid_t, lent = lax.optimization_barrier((resid_t, lent))
    preact = dot(enc_weight[0], resid_t, 0, 0) + enc_bias[0][:, None]
    latent = gelu_tanh(preact).astype(jnp.bfloat16)
    lent_latent = lax.ppermute(latent, LAYER, [(0, 1), (1, 0), (2, 3), (3, 2)])

    sums = decode(dec, lent, latent, lent_latent)
    parts = lax.all_to_all(sums.reshape(2 * lats, own_rows, tokens), SAME_CORE, 0, 0, tiled=True)
    recon = jnp.sum(parts.astype(jnp.float32), axis=0)

    error = recon + dec_bias[0][:, None] - target[0].T.astype(jnp.float32)
    grad_dec_bias = (factor * jnp.sum(error, axis=1))[None]
    out_grad = (factor * error).astype(jnp.bfloat16)

    grads = gather_rows(out_grad, SAME_CORE, 2 * lats).reshape(2, width, tokens)
    other_grads = lax.ppermute(grads, LAYER, [(0, 1), (1, 0), (3, 2)])

    grad_dec, total = backward(dec, latent, grads)
    grad_dec, grad_enc, bias_grad = backward(dec, latent, other_grads, [total, grad_dec], [preact, resid_t])
    return (grad_enc[None], bias_grad, grad_dec[None], grad_dec_bias)


def solution(mesh):
    fine = Mesh(mesh.devices.reshape(2, 2, 2, 4, 4), LAYER + LAT)
    in_specs = (
        P(LAYER, None, LAT),
        P(LAYER, None, LAT),
        P(LAYER, None, LAT),
        P(LAYER, LAT),
        P(LAYER, None, LAT, None),
        P(LAYER, LAT),
    )
    out_specs = (
        P(LAYER, None, LAT),
        P(LAYER, LAT),
        P(LAYER, None, LAT, None),
        P(LAYER, LAT),
    )
    return jax.shard_map(body, mesh=fine, in_specs=in_specs, out_specs=out_specs, check_vma=False)
```

```python
import math

import jax
import jax.numpy as jnp
from jax import lax
from jax.experimental import pallas as pl
from jax.experimental.pallas import tpu as pltpu
from jax.sharding import Mesh, PartitionSpec as P

LAYER = ("zlo", "core")
LAT = ("zhi", "y", "x")
SAME_CORE = ("zlo", "zhi", "y", "x")
TILE = 1152
ANYWHERE = pl.BlockSpec(memory_space=pl.ANY)
LOCAL = pl.BlockSpec(memory_space=pltpu.VMEM)
PARAMS = pltpu.CompilerParams(vmem_limit_bytes=14 * 1024 * 1024)


def gelu_tanh(values):
    return jax.nn.gelu(values, approximate=True)


def gelu_slope(x):
    scale, cubic = math.sqrt(2.0 / math.pi), 0.044715
    bent = jnp.tanh(scale * (x + cubic * x * x * x))
    return 0.5 * (1.0 + bent) + 0.5 * x * (1.0 - bent * bent) * scale * (1.0 + 3.0 * cubic * x * x)


def dot(a, b, ca, cb):
    return lax.dot_general(a, b, (((ca,), (cb,)), ((), ())), preferred_element_type=jnp.float32)


def gather_rows(block, axes, count):
    copies = jnp.broadcast_to(block[None], (count,) + block.shape)
    return lax.all_to_all(copies, axes, 0, 0, tiled=True)


def buffers(count, *shape):
    return [pltpu.VMEM((count,) + shape, jnp.bfloat16), pltpu.SemaphoreType.DMA((count,))]


def place():
    return lax.axis_index("zlo"), lax.axis_index("core")


def decode(dec, lent, latent, lent_latent):
    _, rows, width = dec.shape
    tokens = latent.shape[1]
    tiles = width // TILE
    steps = 2 * tiles

    def kernel(dec_ref, lent_ref, latent_ref, lent_latent_ref, sums_ref):
        zlo, core = place()

        def live(step):
            return (zlo == 0) | (step >= tiles)

        def lent_live(step):
            return (core == 1) | (zlo == 0) if step >= tiles else (core == 1) & (zlo == 0)

        def columns(step):
            return pl.ds(step % tiles * TILE, TILE)

        def product(ref, latent_ref, step):
            return dot(ref[core + 2 * (step // tiles), :, columns(step)], latent_ref[...], 0, 0)

        for step in range(steps):
            @pl.when(live(step) & lent_live(step))
            def _(step=step):
                both = product(dec_ref, latent_ref, step) + product(lent_ref, lent_latent_ref, step)
                sums_ref[step // tiles, columns(step)] = both.astype(jnp.bfloat16)

            @pl.when(live(step) & jnp.logical_not(lent_live(step)))
            def _(step=step):
                sums_ref[step // tiles, columns(step)] = product(dec_ref, latent_ref, step).astype(jnp.bfloat16)

            @pl.when(jnp.logical_not(live(step)))
            def _(step=step):
                sums_ref[step // tiles, columns(step)] = jnp.zeros((TILE, tokens), jnp.bfloat16)

    return pl.pallas_call(
        kernel,
        in_specs=[LOCAL, LOCAL, LOCAL, LOCAL],
        out_specs=LOCAL,
        out_shape=jax.ShapeDtypeStruct((2, width, tokens), jnp.bfloat16),
        compiler_params=PARAMS,
        cost_estimate=pl.CostEstimate(
            flops=8 * rows * width * tokens, bytes_accessed=12 * rows * width, transcendentals=0),
        name="decode",
    )(dec, lent, latent, lent_latent)


def backward(dec, latent, grads, given=None, finish=None):
    _, rows, width = dec.shape
    tokens = latent.shape[1]
    tiles = width // TILE
    steps = 2 * tiles
    given = given or []
    n_given = len(given)

    def kernel(dec_ref, latent_ref, grads_ref, *refs):
        zlo, core = place()
        first_target = 1 - core if given else core
        given_refs, refs = refs[:n_given], refs[n_given:]
        if finish:
            preact_ref, resid_ref, grad_dec_ref, grad_enc_ref, bias_ref, *refs = refs
            total_ref, enc_buf, enc_sem, *refs = refs
        else:
            grad_dec_ref, total_ref, *refs = refs
        out_buf, out_sem = refs

        def target(step):
            return first_target + 2 * (step // tiles)

        def live(step):
            return target(step) >= 2 * zlo + core

        def columns(step):
            return pl.ds(step % tiles * TILE, TILE)

        def out_copy(step):
            block = grad_dec_ref.at[target(step), :, columns(step)]
            return pltpu.make_async_copy(out_buf.at[step], block, out_sem.at[step])

        def enc_copy(part):
            return pltpu.make_async_copy(enc_buf.at[part], grad_enc_ref.at[columns(part)], enc_sem.at[part])

        total_ref[...] = given_refs[0][...] if given else jnp.zeros_like(total_ref)
        for step in range(steps):
            @pl.when(live(step))
            def _(step=step):
                grad = grads_ref[step // tiles, columns(step), :]
                total_ref[...] += dot(dec_ref[target(step), :, columns(step)], grad, 1, 0)
                out_buf[step] = dot(latent_ref[...], grad, 1, 1).astype(jnp.bfloat16)

            @pl.when(jnp.logical_not(live(step)))
            def _(step=step):
                out_buf[step] = jnp.zeros((rows, TILE), jnp.bfloat16)

            out_copy(step).start()
        if finish:
            pre_grad = total_ref[...] * gelu_slope(preact_ref[...])
            bias_ref[...] = jnp.sum(pre_grad.T, axis=0, keepdims=True)
            pre_grad = pre_grad.astype(jnp.bfloat16)
            for part in range(tiles):
                enc_buf[part] = dot(resid_ref[columns(part), :], pre_grad, 1, 1).astype(jnp.bfloat16)
                enc_copy(part).start()
        for step in range(steps):
            out_copy(step).wait()
        if finish:
            for part in range(tiles):
                enc_copy(part).wait()

    operands = [dec, latent, grads, *given]
    in_specs = [LOCAL, LOCAL, LOCAL] + [LOCAL, ANYWHERE][:n_given]
    out_shape = [jax.ShapeDtypeStruct(dec.shape, jnp.bfloat16)]
    out_specs = [ANYWHERE]
    scratch = []
    if finish:
        operands += finish
        in_specs += [LOCAL, LOCAL]
        out_shape += [jax.ShapeDtypeStruct((width, rows), jnp.bfloat16), jax.ShapeDtypeStruct((1, rows), jnp.float32)]
        out_specs += [ANYWHERE, LOCAL]
        scratch = [pltpu.VMEM((rows, tokens), jnp.float32)] + buffers(tiles, TILE, rows)
    else:
        out_shape += [jax.ShapeDtypeStruct((rows, tokens), jnp.float32)]
        out_specs += [LOCAL]
    scratch += buffers(steps, rows, TILE)
    return pl.pallas_call(
        kernel,
        in_specs=in_specs,
        out_specs=out_specs,
        scratch_shapes=scratch,
        out_shape=out_shape,
        input_output_aliases={4: 0} if given else {},
        compiler_params=PARAMS,
        cost_estimate=pl.CostEstimate(
            flops=8 * rows * width * tokens, bytes_accessed=12 * rows * width, transcendentals=0),
        name="other_targets" if given else "own_targets",
    )(*operands)


def body(resid, target, enc_weight, enc_bias, dec_weight, dec_bias):
    tokens = resid.shape[1]
    own_rows = resid.shape[2]
    lats = lax.axis_size("zhi") * lax.axis_size("y") * lax.axis_size("x")
    width = own_rows * lats
    factor = 2.0 / tokens
    dec = dec_weight[0]

    lent = lax.ppermute(dec, LAYER, [(0, 1), (1, 0), (2, 3)])

    resid_t = gather_rows(resid[0].T, LAT, lats).reshape(width, tokens)
    resid_t, lent = lax.optimization_barrier((resid_t, lent))
    preact = dot(enc_weight[0], resid_t, 0, 0) + enc_bias[0][:, None]
    latent = gelu_tanh(preact).astype(jnp.bfloat16)
    lent_latent = lax.ppermute(latent, LAYER, [(0, 1), (1, 0), (2, 3), (3, 2)])

    sums = decode(dec, lent, latent, lent_latent)
    parts = lax.all_to_all(sums.reshape(2 * lats, own_rows, tokens), SAME_CORE, 0, 0, tiled=True)
    recon = jnp.sum(parts.astype(jnp.float32), axis=0)

    error = recon + dec_bias[0][:, None] - target[0].T.astype(jnp.float32)
    grad_dec_bias = (factor * jnp.sum(error, axis=1))[None]
    out_grad = (factor * error).astype(jnp.bfloat16)

    grads = gather_rows(out_grad, SAME_CORE, 2 * lats).reshape(2, width, tokens)
    other_grads = lax.ppermute(grads, LAYER, [(0, 1), (1, 0), (3, 2)])

    grad_dec, total = backward(dec, latent, grads)
    grad_dec, grad_enc, bias_grad = backward(dec, latent, other_grads, [total, grad_dec], [preact, resid_t])
    return (grad_enc[None], bias_grad, grad_dec[None], grad_dec_bias)


def solution(mesh):
    fine = Mesh(mesh.devices.reshape(2, 2, 2, 4, 4), LAYER + LAT)
    in_specs = (
        P(LAYER, None, LAT),
        P(LAYER, None, LAT),
        P(LAYER, None, LAT),
        P(LAYER, LAT),
        P(LAYER, None, LAT, None),
        P(LAYER, LAT),
    )
    out_specs = (
        P(LAYER, None, LAT),
        P(LAYER, LAT),
        P(LAYER, None, LAT, None),
        P(LAYER, LAT),
    )
    return jax.shard_map(body, mesh=fine, in_specs=in_specs, out_specs=out_specs, check_vma=False)
```

```python
import math

import jax
import jax.numpy as jnp
from jax import lax
from jax.experimental import pallas as pl
from jax.experimental.pallas import tpu as pltpu
from jax.sharding import Mesh, PartitionSpec as P

LAYER = ("zlo", "core")
LAT = ("zhi", "y", "x")
SAME_CORE = ("zlo", "zhi", "y", "x")
TILE = 2304
ANYWHERE = pl.BlockSpec(memory_space=pl.ANY)
LOCAL = pl.BlockSpec(memory_space=pltpu.VMEM)
PARAMS = pltpu.CompilerParams(vmem_limit_bytes=14 * 1024 * 1024)


def gelu_tanh(values):
    return jax.nn.gelu(values, approximate=True)


def gelu_slope(x):
    scale, cubic = math.sqrt(2.0 / math.pi), 0.044715
    bent = jnp.tanh(scale * (x + cubic * x * x * x))
    return 0.5 * (1.0 + bent) + 0.5 * x * (1.0 - bent * bent) * scale * (1.0 + 3.0 * cubic * x * x)


def dot(a, b, ca, cb):
    return lax.dot_general(a, b, (((ca,), (cb,)), ((), ())), preferred_element_type=jnp.float32)


def gather_rows(block, axes, count):
    copies = jnp.broadcast_to(block[None], (count,) + block.shape)
    return lax.all_to_all(copies, axes, 0, 0, tiled=True)


def buffers(count, *shape):
    return [pltpu.VMEM((count,) + shape, jnp.bfloat16), pltpu.SemaphoreType.DMA((count,))]


def place():
    return lax.axis_index("zlo"), lax.axis_index("core")


def decode(dec, lent, latent, lent_latent):
    _, rows, width = dec.shape
    tokens = latent.shape[1]
    tiles = width // TILE
    steps = 2 * tiles

    def kernel(dec_ref, lent_ref, latent_ref, lent_latent_ref, sums_ref):
        zlo, core = place()

        def live(step):
            return (zlo == 0) | (step >= tiles)

        def lent_live(step):
            return (core == 1) | (zlo == 0) if step >= tiles else (core == 1) & (zlo == 0)

        def columns(step):
            return pl.ds(step % tiles * TILE, TILE)

        def product(ref, latent_ref, step):
            return dot(ref[core + 2 * (step // tiles), :, columns(step)], latent_ref[...], 0, 0)

        for step in range(steps):
            @pl.when(live(step) & lent_live(step))
            def _(step=step):
                both = product(dec_ref, latent_ref, step) + product(lent_ref, lent_latent_ref, step)
                sums_ref[step // tiles, columns(step)] = both.astype(jnp.bfloat16)

            @pl.when(live(step) & jnp.logical_not(lent_live(step)))
            def _(step=step):
                sums_ref[step // tiles, columns(step)] = product(dec_ref, latent_ref, step).astype(jnp.bfloat16)

            @pl.when(jnp.logical_not(live(step)))
            def _(step=step):
                sums_ref[step // tiles, columns(step)] = jnp.zeros((TILE, tokens), jnp.bfloat16)

    return pl.pallas_call(
        kernel,
        in_specs=[LOCAL, LOCAL, LOCAL, LOCAL],
        out_specs=LOCAL,
        out_shape=jax.ShapeDtypeStruct((2, width, tokens), jnp.bfloat16),
        compiler_params=PARAMS,
        cost_estimate=pl.CostEstimate(
            flops=8 * rows * width * tokens, bytes_accessed=12 * rows * width, transcendentals=0),
        name="decode",
    )(dec, lent, latent, lent_latent)


def backward(dec, latent, grads, given=None, finish=None):
    _, rows, width = dec.shape
    tokens = latent.shape[1]
    tiles = width // TILE
    steps = 2 * tiles
    given = given or []
    n_given = len(given)

    def kernel(dec_ref, latent_ref, grads_ref, *refs):
        zlo, core = place()
        first_target = 1 - core if given else core
        given_refs, refs = refs[:n_given], refs[n_given:]
        if finish:
            preact_ref, resid_ref, grad_dec_ref, grad_enc_ref, bias_ref, *refs = refs
            total_ref, enc_buf, enc_sem, *refs = refs
        else:
            grad_dec_ref, total_ref, *refs = refs
        out_buf, out_sem = refs

        def target(step):
            return first_target + 2 * (step // tiles)

        def live(step):
            return target(step) >= 2 * zlo + core

        def columns(step):
            return pl.ds(step % tiles * TILE, TILE)

        def out_copy(step):
            block = grad_dec_ref.at[target(step), :, columns(step)]
            return pltpu.make_async_copy(out_buf.at[step], block, out_sem.at[step])

        def enc_copy(part):
            return pltpu.make_async_copy(enc_buf.at[part], grad_enc_ref.at[columns(part)], enc_sem.at[part])

        total_ref[...] = given_refs[0][...] if given else jnp.zeros_like(total_ref)
        for step in range(steps):
            @pl.when(live(step))
            def _(step=step):
                grad = grads_ref[step // tiles, columns(step), :]
                total_ref[...] += dot(dec_ref[target(step), :, columns(step)], grad, 1, 0)
                out_buf[step] = dot(latent_ref[...], grad, 1, 1).astype(jnp.bfloat16)

            @pl.when(jnp.logical_not(live(step)))
            def _(step=step):
                out_buf[step] = jnp.zeros((rows, TILE), jnp.bfloat16)

            out_copy(step).start()
        if finish:
            pre_grad = total_ref[...] * gelu_slope(preact_ref[...])
            bias_ref[...] = jnp.sum(pre_grad.T, axis=0, keepdims=True)
            pre_grad = pre_grad.astype(jnp.bfloat16)
            for part in range(tiles):
                enc_buf[part] = dot(resid_ref[columns(part), :], pre_grad, 1, 1).astype(jnp.bfloat16)
                enc_copy(part).start()
        for step in range(steps):
            out_copy(step).wait()
        if finish:
            for part in range(tiles):
                enc_copy(part).wait()

    operands = [dec, latent, grads, *given]
    in_specs = [LOCAL, LOCAL, LOCAL] + [LOCAL, ANYWHERE][:n_given]
    out_shape = [jax.ShapeDtypeStruct(dec.shape, jnp.bfloat16)]
    out_specs = [ANYWHERE]
    scratch = []
    if finish:
        operands += finish
        in_specs += [LOCAL, LOCAL]
        out_shape += [jax.ShapeDtypeStruct((width, rows), jnp.bfloat16), jax.ShapeDtypeStruct((1, rows), jnp.float32)]
        out_specs += [ANYWHERE, LOCAL]
        scratch = [pltpu.VMEM((rows, tokens), jnp.float32)] + buffers(tiles, TILE, rows)
    else:
        out_shape += [jax.ShapeDtypeStruct((rows, tokens), jnp.float32)]
        out_specs += [LOCAL]
    scratch += buffers(steps, rows, TILE)
    return pl.pallas_call(
        kernel,
        in_specs=in_specs,
        out_specs=out_specs,
        scratch_shapes=scratch,
        out_shape=out_shape,
        input_output_aliases={4: 0} if given else {},
        compiler_params=PARAMS,
        cost_estimate=pl.CostEstimate(
            flops=8 * rows * width * tokens, bytes_accessed=12 * rows * width, transcendentals=0),
        name="other_targets" if given else "own_targets",
    )(*operands)


def body(resid, target, enc_weight, enc_bias, dec_weight, dec_bias):
    tokens = resid.shape[1]
    own_rows = resid.shape[2]
    lats = lax.axis_size("zhi") * lax.axis_size("y") * lax.axis_size("x")
    width = own_rows * lats
    factor = 2.0 / tokens
    dec = dec_weight[0]

    lent = lax.ppermute(dec, LAYER, [(0, 1), (1, 0), (2, 3)])

    resid_t = gather_rows(resid[0].T, LAT, lats).reshape(width, tokens)
    resid_t, lent = lax.optimization_barrier((resid_t, lent))
    preact = dot(enc_weight[0], resid_t, 0, 0) + enc_bias[0][:, None]
    latent = gelu_tanh(preact).astype(jnp.bfloat16)
    lent_latent = lax.ppermute(latent, LAYER, [(0, 1), (1, 0), (2, 3), (3, 2)])

    sums = decode(dec, lent, latent, lent_latent)
    parts = lax.all_to_all(sums.reshape(2 * lats, own_rows, tokens), SAME_CORE, 0, 0, tiled=True)
    recon = jnp.sum(parts.astype(jnp.float32), axis=0)

    error = recon + dec_bias[0][:, None] - target[0].T.astype(jnp.float32)
    grad_dec_bias = (factor * jnp.sum(error, axis=1))[None]
    out_grad = (factor * error).astype(jnp.bfloat16)

    grads = gather_rows(out_grad, SAME_CORE, 2 * lats).reshape(2, width, tokens)
    other_grads = lax.ppermute(grads, LAYER, [(0, 1), (1, 0), (3, 2)])

    grad_dec, total = backward(dec, latent, grads)
    grad_dec, grad_enc, bias_grad = backward(dec, latent, other_grads, [total, grad_dec], [preact, resid_t])
    return (grad_enc[None], bias_grad, grad_dec[None], grad_dec_bias)


def solution(mesh):
    fine = Mesh(mesh.devices.reshape(2, 2, 2, 4, 4), LAYER + LAT)
    in_specs = (
        P(LAYER, None, LAT),
        P(LAYER, None, LAT),
        P(LAYER, None, LAT),
        P(LAYER, LAT),
        P(LAYER, None, LAT, None),
        P(LAYER, LAT),
    )
    out_specs = (
        P(LAYER, None, LAT),
        P(LAYER, LAT),
        P(LAYER, None, LAT, None),
        P(LAYER, LAT),
    )
    return jax.shard_map(body, mesh=fine, in_specs=in_specs, out_specs=out_specs, check_vma=False)
```
